256 devices in a mesh: rep: 4 (over x_hi, core), fsdp: 64 (over y, x_lo, z).
Axes of the slice: x: 4 (x_hi: 2, x_lo: 2; x = x_hi * 2 + x_lo), y: 4, z: 8, core: 2. Of those that a mesh axis runs over, the one named last changes fastest.
Arguments:
- acts: bfloat16 [4, 16384, 8192], P('rep', 'fsdp'), may hold values from -16 to 16
- out_grad: bfloat16 [4, 16384, 512], P('rep', 'fsdp'), may hold values from -6 to 6
- weights: bfloat16 [4, 8192, 512], P('rep', 'fsdp'), may hold values from -0.0625 to 0.0625
- anchor: float32 [8192, 512], P('fsdp', 'rep'), may hold values from -0.0625 to 0.0625
- momentum: float32 [8192, 512], P('fsdp', 'rep'), may hold values from -0.078125 to 0.078125
- plan: int32 [4], replicated, may hold values 0 or 1
Outputs:
- values: bfloat16 [4, 16384, 512], P('rep', 'fsdp')
- act_grad: bfloat16 [4, 16384, 8192], P('rep', 'fsdp')
- new_weights: bfloat16 [4, 8192, 512], P('rep', 'fsdp')
- new_momentum: float32 [8192, 512], P('fsdp', 'rep')
The draws below stay inside these ranges and needn't reach their ends.
All inputs are finite; a program needn't handle non-finite values.
Results may differ from the reference program's by a relative error of at most 0.001.
Values may be sent and summed in bfloat16 or wider, within the bound.
No kernel may reach another device: no remote copies, remote signals or barrier semaphores. Data moves between devices by JAX's collectives and lax.ppermute only.
A program may use at most 128 MiB of HBM per device.

```python
import math
import jax
import jax.numpy as jnp

D = 8192
HEADS_W = 4
HEAD_DIM = 128
KVW = 512
TOKENS = 16384
N_REP = 4


def plant(array, rng, smallest, top_value):
    spot = [jax.random.randint(jax.random.fold_in(rng, axis), (), 0, length) for axis, length in enumerate(array.shape)]
    main_axis = array.shape.index(max(array.shape))
    neighbour = spot[:main_axis] + [(spot[main_axis] + 1) % array.shape[main_axis]] + spot[main_axis + 1:]
    return array.at[tuple(spot)].set(smallest).at[tuple(neighbour)].set(top_value)


def with_spikes(values, rng, source, target, shards_of, factor):
    owner, partner = [(jnp.arange(values.shape[dim]) // (values.shape[dim] // shards_of)).reshape([-1 if axis == dim else 1 for axis in range(values.ndim)]) for dim in (source, target)]
    chosen = jax.random.permutation(rng, shards_of)[partner]
    strong = (owner == chosen) | (owner == (partner + shards_of // 2) % shards_of)
    return jnp.where(strong, factor * values, values)


def level_of(rng, extent, cuts, low, high):
    level, own = 1.0, jax.random.fold_in(rng, 6)
    for axis_at, shards_of in cuts:
        draws = jnp.exp(jax.random.uniform(jax.random.fold_in(own, axis_at), (shards_of,), jnp.float32, low / len(cuts), high / len(cuts)))
        level = level * jnp.repeat(draws, extent[axis_at] // shards_of).reshape([-1 if axis == axis_at else 1 for axis in range(len(extent))])
    return level


def bell_draw(rng, dims, width, reach, split=(), dtype=jnp.bfloat16):
    loudness = level_of(rng, dims, split, -0.22, 0.18) if split else 1.0
    drawn = jax.random.normal(rng, dims, jnp.float32) * width * loudness
    return jnp.minimum(jnp.maximum(drawn, -reach), reach).astype(dtype)


def heavy_noise(stream_key, shape, deviation, most, pieces, heavy, dtype=jnp.bfloat16):
    drawn = deviation * jax.random.normal(stream_key, shape, jnp.float32)
    if pieces:
        drawn = drawn * level_of(stream_key, shape, pieces, -0.22, 0.18)
    return jnp.clip(with_spikes(drawn, jax.random.fold_in(stream_key, 3), *heavy), -most, most).astype(dtype)


def setup_inputs(seed: int = 0) -> dict:
    key_list = jax.random.split(jax.random.key(seed), 7)
    return {
        "acts": heavy_noise(key_list[0], (N_REP, TOKENS, D), 1.0, 16.0, ((0, 4), (1, 64)), (1, 2, 64, 4.0)),
        "out_grad": bell_draw(key_list[1], (N_REP, TOKENS, KVW), 1.0, 6.0, ((0, 4), (1, 64))),
        "weights": bell_draw(key_list[2], (N_REP, D, KVW), D ** -0.5, 0.0625, ((0, 4), (1, 64))),
        "anchor": bell_draw(key_list[3], (D, KVW), D ** -0.5, 0.0625, ((0, 64), (1, 4)), jnp.float32),
        "momentum": bell_draw(key_list[4], (D, KVW), (0.5 * D ** -0.5), 0.078125, ((0, 64), (1, 4)), jnp.float32),
        "plan": plant((jax.random.randint(key_list[5], (HEADS_W,), 0, 2) < 1).astype(jnp.int32), jax.random.fold_in(key_list[5], 1), 0, 1),
    }


outer_rate = 0.7
momentum_coef = 0.9

def reference(acts, out_grad, weights, anchor, momentum, plan):
    inner_rate = 1.0 / math.sqrt(TOKENS * D)
    value_list = []
    grad_list = []
    inner_list = []
    for group in range(N_REP):
        value_list.append(jnp.dot(acts[group], weights[group], preferred_element_type=jnp.float32).astype(jnp.bfloat16))
        grad_list.append(jnp.dot(out_grad[group], weights[group].T, preferred_element_type=jnp.float32).astype(jnp.bfloat16))
        weight_grad = jnp.dot(acts[group].T, out_grad[group], preferred_element_type=jnp.float32)
        inner_list.append(weights[group].astype(jnp.float32) - inner_rate * weight_grad)
    group_total = inner_list[0]
    for group in range(1, N_REP):
        group_total = group_total + inner_list[group]
    group_mean = group_total / N_REP
    pseudo_grad = anchor - group_mean
    mom_next = momentum_coef * momentum + pseudo_grad
    outer_weight = anchor - outer_rate * (pseudo_grad + momentum_coef * mom_next)
    col_mask = jnp.repeat(plan, HEAD_DIM) > 0
    outer_bf = outer_weight.astype(jnp.bfloat16)
    new_list = [jnp.where(col_mask[None, :], outer_bf, inner_weight.astype(jnp.bfloat16)) for inner_weight in inner_list]
    new_momentum = jnp.where(col_mask[None, :], mom_next, momentum)
    return (jnp.stack(value_list), jnp.stack(grad_list), jnp.stack(new_list), new_momentum)
```

```python
import functools
import math

import jax
import jax.numpy as jnp
from jax import lax
from jax.experimental import pallas as pl
from jax.experimental.pallas import tpu as pltpu
from jax.sharding import Mesh, PartitionSpec as P

outer_rate = 0.7
momentum_coef = 0.9
NY, NX, NZ = 4, 2, 8
SUB = NY * NX
REP = ("xh", "core")
FSDP = ("y", "xl", "z")
ANY = pl.BlockSpec(memory_space=pl.ANY)
F32 = jnp.float32
BF16 = jnp.bfloat16


def shift_z(x, dz):
    return lax.ppermute(x, "z", [(i, (i + dz) % NZ) for i in range(NZ)])


def shift_yx(x, dy, dx):
    pairs = [
        (y * NX + c, (y + dy) % NY * NX + (c ^ dx)) for y in range(NY) for c in range(NX)
    ]
    return lax.ppermute(x, ("y", "xl"), pairs)


def grad_kernel(place_ref, own_ref, *refs):
    blocks, grads_ref, out_ref = (own_ref,) + refs[: SUB - 1], refs[SUB - 1], refs[SUB]
    total = None
    for k, block in enumerate(blocks):
        term = lax.dot_general(
            block[...],
            grads_ref[place_ref[NZ * 2 + k]],
            (((0,), (0,)), ((), ())),
            preferred_element_type=F32,
        )
        total = term if total is None else total + term
    out_ref[0] = total


def partial_grad(tokens, received, grads, place):
    width = received[0].shape[1] // NZ
    rows = tokens.shape[0]
    heads = grads.shape[2]
    grid_spec = pltpu.PrefetchScalarGridSpec(
        num_scalar_prefetch=1,
        grid=(NZ,),
        in_specs=[pl.BlockSpec((rows, width), lambda d, p: (0, p[d]))]
        + [pl.BlockSpec((rows, width), lambda d, p: (0, p[NZ + d]))] * (SUB - 1)
        + [pl.BlockSpec(grads.shape, lambda d, p: (0, 0, 0))],
        out_specs=pl.BlockSpec((1, width, heads), lambda d, p: (d, 0, 0)),
    )
    return pl.pallas_call(
        grad_kernel,
        grid_spec=grid_spec,
        out_shape=jax.ShapeDtypeStruct((NZ, width, heads), F32),
        compiler_params=pltpu.CompilerParams(vmem_limit_bytes=32 << 20),
        cost_estimate=pl.CostEstimate(
            flops=2 * SUB * rows * NZ * width * heads,
            bytes_accessed=SUB * rows * NZ * width * 2 + NZ * width * heads * 4,
            transcendentals=0,
        ),
        name="partial_grad",
    )(place, tokens, *received, grads)


def project_kernel(sizes, first, last, place_ref, tokens_ref, grads_ref, *refs):
    n = len(sizes)
    weight_refs, refs = refs[:n], refs[n:]
    if not first:
        sum_ref, _, refs = refs[0], refs[1], refs[2:]
    sum_out, grad_out, token_buf, grad_buf, in_sem, out_sem = refs
    width = token_buf.shape[2] // NX
    rows = token_buf.shape[1]
    pieces = [(i, j) for i, size in enumerate(sizes) for j in range(size)]

    def columns(k, c):
        return pl.ds(pl.multiple_of((place_ref[k] + c * NZ) * width, width), width)

    def fetch(k, c):
        return pltpu.make_async_copy(
            tokens_ref.at[:, columns(k, c)],
            token_buf.at[k, :, pl.ds(c * width, width)],
            in_sem.at[k, c],
        )

    def put(k, c):
        return pltpu.make_async_copy(
            grad_buf.at[k, :, pl.ds(c * width, width)],
            grad_out.at[:, columns(k, c)],
            out_sem.at[k, c],
        )

    for k in range(len(pieces)):
        for c in range(NX):
            fetch(k, c).start()
    grads = grads_ref[...]
    total = None if first else sum_ref[...]
    for k, (i, j) in enumerate(pieces):
        weight = weight_refs[i][pl.ds(j * NX * width, NX * width), :]
        grad_buf[k] = lax.dot_general(
            grads, weight, (((1,), (1,)), ((), ())), preferred_element_type=F32
        ).astype(BF16)
        for c in range(NX):
            put(k, c).start()
        for c in range(NX):
            fetch(k, c).wait()
        term = jnp.dot(token_buf[k], weight, preferred_element_type=F32)
        total = term if total is None else total + term
    sum_out[...] = total.astype(sum_out.dtype)
    for k in range(len(pieces)):
        for c in range(NX):
            put(k, c).wait()


def project(tokens, grads, weights, place, state, last):
    rows, heads = grads.shape
    width = tokens.shape[1] // (NY * NX * NZ)
    pair = NX * width
    sizes = tuple(w.shape[0] // pair for w in weights)
    count = sum(sizes)
    first = state is None
    whole = pl.BlockSpec(memory_space=pltpu.VMEM)
    n_in = 3 + len(weights)
    return pl.pallas_call(
        functools.partial(project_kernel, sizes, first, last),
        in_specs=[pl.BlockSpec(memory_space=pltpu.SMEM), ANY, whole]
        + [whole] * len(weights)
        + ([] if first else [whole, ANY]),
        out_specs=(whole, ANY),
        out_shape=(
            jax.ShapeDtypeStruct((rows, heads), BF16 if last else F32),
            jax.ShapeDtypeStruct(tokens.shape, BF16),
        ),
        scratch_shapes=[
            pltpu.VMEM((count, rows, pair), BF16),
            pltpu.VMEM((count, rows, pair), BF16),
            pltpu.SemaphoreType.DMA((count, NX)),
            pltpu.SemaphoreType.DMA((count, NX)),
        ],
        input_output_aliases={} if first else {n_in + 1: 1},
        compiler_params=pltpu.CompilerParams(vmem_limit_bytes=24 << 20),
        cost_estimate=pl.CostEstimate(
            flops=4 * rows * heads * count * pair,
            bytes_accessed=count * pair * (rows * 4 + heads * 2),
            transcendentals=0,
        ),
        name="project",
    )(place, tokens, grads, *weights, *(() if first else state))


def outer_kernel(plan_ref, rank_ref, near_ref, far_ref, inner_ref, state_ref, new_ref, mom_ref):
    width = mom_ref.shape[1]
    groups = state_ref.shape[0]

    def step(at, columns):
        anchor, momentum = state_ref[at, 0], state_ref[at, 1]
        mean = (near_ref[:, columns] + far_ref[:, columns]) / groups
        pseudo = anchor - mean
        return anchor, momentum, pseudo, momentum_coef * momentum + pseudo

    per_head = plan_ref.shape[0]
    for b in range(per_head):
        columns = pl.ds(b * width, width)
        anchor, _, pseudo, following = step(b, columns)
        outer = anchor - outer_rate * (pseudo + momentum_coef * following)
        synced = jnp.full(outer.shape, plan_ref[b], jnp.int32) > 0
        new_ref[:, columns] = jnp.where(synced, outer, inner_ref[:, columns]).astype(BF16)
    rank = rank_ref[0]
    columns = pl.ds(pl.multiple_of(rank * width, width), width)
    _, momentum, _, following = step(rank, columns)
    synced = jnp.full(momentum.shape, plan_ref[rank], jnp.int32) > 0
    mom_ref[...] = jnp.where(synced, following, momentum)


def outer_step(plan, rank, near, far, inner, state):
    smem = pl.BlockSpec(memory_space=pltpu.SMEM)
    whole = pl.BlockSpec(memory_space=pltpu.VMEM)
    return pl.pallas_call(
        outer_kernel,
        in_specs=[smem, smem, whole, whole, whole, whole],
        out_specs=(whole, whole),
        out_shape=(
            jax.ShapeDtypeStruct(inner.shape, BF16),
            jax.ShapeDtypeStruct(state.shape[2:], F32),
        ),
        name="outer_step",
    )(plan, rank, near, far, inner, state)


def local(acts, out_grad, weights, anchor, momentum, plan):
    tokens, grads_out, local_weight = acts[0], out_grad[0], weights[0]
    rows, depth = tokens.shape
    total_tokens = rows * NY * NX * NZ
    inner_rate = 1.0 / math.sqrt(total_tokens * depth)
    y, c, z = lax.axis_index("y"), lax.axis_index("xl"), lax.axis_index("z")
    rank = lax.axis_index(REP)
    part = depth // SUB

    block = lax.all_gather(local_weight, ("y", "xl"), axis=0, tiled=True)
    grads = lax.all_gather(grads_out, ("y", "xl"), axis=0, tiled=False)
    state = lax.all_gather(jnp.stack([anchor, momentum]), REP, axis=0, tiled=False)

    received, owners = [], [y * NX + c]
    for dy, dx in [(2, 1), (1, 1), (3, 1), (2, 0), (1, 0), (3, 0), (0, 1)]:
        to = (y + dy) % NY * NX + (c ^ dx)
        piece = lax.dynamic_slice(tokens, (0, to * part), (rows, part))
        received.append(shift_yx(piece, dy, dx))
        owners.append((y - dy) % NY * NX + (c ^ dx))
    relative = [(z + d) % NZ for d in range(NZ)]
    place = jnp.stack([(y * NX + c) * NZ + r for r in relative] + relative + owners)
    terms = partial_grad(tokens, received, grads, place.astype(jnp.int32))

    half = terms.shape[1] // 2
    right = shift_z(terms[4, :half], 1)
    left = shift_z(terms[4, half:], -1)
    right = jnp.concatenate([terms[3, :half] + right, terms[3, half:]])
    left = jnp.concatenate([terms[5, :half], terms[5, half:] + left])
    for d in (2, 1):
        right, left = shift_z(right, 1), shift_z(left, -1)
        right, left = terms[d] + right, terms[NZ - d] + left
    right, left = shift_z(right, 1), shift_z(left, -1)
    inner = local_weight.astype(F32) - inner_rate * (terms[0] + right + left)

    def places(dz, ys=range(NY)):
        return [v * (NX * NZ) + (z + dz) % NZ for v in ys]

    def at(*lists):
        return jnp.stack(sum(lists, [])).astype(jnp.int32)

    carry = project(tokens, grads_out, [block], at(places(0)), None, False)
    right = left = block
    for k in (1, 2, 3):
        right, left = shift_z(right, 1), shift_z(left, -1)
        carry = project(
            tokens, grads_out, [right, left], at(places(-k), places(k)), carry, False
        )
    half = block.shape[0] // 2
    right, left = shift_z(right[:half], 1), shift_z(left[half:], -1)
    values, act_grad = project(
        tokens, grads_out, [right, left], at(places(4)), carry, True
    )

    near = inner + lax.ppermute(inner, "core", [(0, 1), (1, 0)])
    far = lax.ppermute(near, "xh", [(0, 1), (1, 0)])
    new_weight, new_momentum = outer_step(
        plan, jnp.reshape(rank, (1,)).astype(jnp.int32), near, far, inner, state
    )
    return values[None], act_grad[None], new_weight[None], new_momentum


def solution(mesh):
    fine = Mesh(mesh.devices.reshape(2, 2, NY, NX, NZ), ("xh", "core", "y", "xl", "z"))
    placed = (
        P(REP, FSDP, None),
        P(REP, FSDP, None),
        P(REP, FSDP, None),
        P(FSDP, REP),
        P(FSDP, REP),
        P(),
    )
    return jax.shard_map(
        local,
        mesh=fine,
        in_specs=placed,
        out_specs=(
            P(REP, FSDP, None),
            P(REP, FSDP, None),
            P(REP, FSDP, None),
            P(FSDP, REP),
        ),
        check_vma=False,
    )
```

```python
import functools
import math

import jax
import jax.numpy as jnp
from jax import lax
from jax.experimental import pallas as pl
from jax.experimental.pallas import tpu as pltpu
from jax.sharding import Mesh, PartitionSpec as P

outer_rate = 0.7
momentum_coef = 0.9
NY, NX, NZ = 4, 2, 8
SUB = NY * NX
REP = ("xh", "core")
FSDP = ("y", "xl", "z")
HBM = pl.BlockSpec(memory_space=pltpu.HBM)
F32 = jnp.float32
BF16 = jnp.bfloat16
STAGES = ((4, 3, 5), (2, 6, 1, 7, 0))


def shift_z(x, dz):
    return lax.ppermute(x, "z", [(i, (i + dz) % NZ) for i in range(NZ)])


def shift_y(x, dy):
    return lax.ppermute(x, "y", [(i, (i + dy) % NY) for i in range(NY)])


def shift_x(x):
    return lax.ppermute(x, "xl", [(0, 1), (1, 0)])


def shift_core(x):
    return lax.ppermute(x, "core", [(0, 1), (1, 0)])


def shift_far(x):
    return lax.ppermute(x, "xh", [(0, 1), (1, 0)])


def sort_kernel(place_ref, tokens_ref, grads_ref, *refs):
    n = len(STAGES)
    outs, (tokens_buf, grads_buf), bufs, (in_sem, out_sem) = (
        refs[:n], refs[n : n + 2], refs[n + 2 : 2 * n + 2], refs[2 * n + 2 :]
    )
    heads = grads_ref.shape[1]
    part = tokens_buf.shape[2]
    width = part // NZ
    fetches = [pltpu.make_async_copy(grads_ref, grads_buf, in_sem.at[SUB])]
    for j in range(SUB):
        fetches.append(
            pltpu.make_async_copy(
                tokens_ref.at[:, pl.ds(j * part, part)], tokens_buf.at[j], in_sem.at[j]
            )
        )
    for fetch in fetches:
        fetch.start()
    fetches[0].wait()
    puts = []
    for j in range(SUB):
        fetches[1 + j].wait()
        bufs[0][j, :, :heads] = grads_buf[...]
        for s, stage in enumerate(STAGES):
            start = heads if s == 0 else 0
            for i, d in enumerate(stage):
                source = pl.multiple_of(place_ref[d] * width, width)
                bufs[s][j, :, pl.ds(start + i * width, width)] = tokens_buf[
                    j, :, pl.ds(source, width)
                ]
            put = pltpu.make_async_copy(bufs[s].at[j], outs[s].at[j], out_sem.at[s, j])
            put.start()
            puts.append(put)
    for put in puts:
        put.wait()


def sort_tokens(tokens, grads, place):
    tokens = pltpu.with_memory_space_constraint(tokens, pltpu.HBM)
    grads = pltpu.with_memory_space_constraint(grads, pltpu.HBM)
    rows, depth = tokens.shape
    heads = grads.shape[1]
    part = depth // SUB
    width = part // NZ
    sizes = [len(stage) * width + (heads if s == 0 else 0) for s, stage in enumerate(STAGES)]
    return pl.pallas_call(
        sort_kernel,
        in_specs=[pl.BlockSpec(memory_space=pltpu.SMEM), HBM, HBM],
        out_specs=(HBM,) * len(sizes),
        out_shape=tuple(pltpu.HBM((SUB, rows, n), tokens.dtype) for n in sizes),
        scratch_shapes=[
            pltpu.VMEM((SUB, rows, part), tokens.dtype),
            pltpu.VMEM((rows, heads), tokens.dtype),
            *[pltpu.VMEM((SUB, rows, n), tokens.dtype) for n in sizes],
            pltpu.SemaphoreType.DMA((SUB + 1,)),
            pltpu.SemaphoreType.DMA((len(sizes), SUB)),
        ],
        compiler_params=pltpu.CompilerParams(vmem_limit_bytes=24 << 20),
        cost_estimate=pl.CostEstimate(
            flops=0, bytes_accessed=4 * rows * (depth + heads), transcendentals=0
        ),
        name="sort_tokens",
    )(place, tokens, grads)


def grad_kernel(tokens_ref, grads_ref, out_ref):
    members, rows, width = tokens_ref.shape
    heads = grads_ref.shape[2]
    out_ref[0] = lax.dot_general(
        tokens_ref[...].reshape(members * rows, width),
        grads_ref[...].reshape(members * rows, heads),
        (((0,), (0,)), ((), ())),
        preferred_element_type=F32,
    )


def partial_grad(tokens, first, heads, width, own):
    members, rows, columns = tokens.shape
    skip = heads // width if own else 0
    count = columns // width - skip
    return pl.pallas_call(
        grad_kernel,
        grid=(count,),
        in_specs=[
            pl.BlockSpec((members, rows, width), lambda d: (0, 0, d + skip)),
            pl.BlockSpec((members, rows, heads), lambda d: (0, 0, 0)),
        ],
        out_specs=pl.BlockSpec((1, width, heads), lambda d: (d, 0, 0)),
        out_shape=jax.ShapeDtypeStruct((count, width, heads), F32),
        compiler_params=pltpu.CompilerParams(vmem_limit_bytes=16 << 20),
        cost_estimate=pl.CostEstimate(flops=0, bytes_accessed=0, transcendentals=0),
        name="partial_grad",
    )(tokens, first)


def project_kernel(sizes, first, last, place_ref, tokens_ref, grads_ref, *refs):
    n = len(sizes)
    weight_refs, refs = refs[:n], refs[n:]
    if not first:
        sum_ref, _, refs = refs[0], refs[1], refs[2:]
    sum_out, grad_out, token_buf, grad_buf, in_sem, out_sem = refs
    width = token_buf.shape[2] // NX
    rows = token_buf.shape[1]
    pieces = [(i, j) for i, size in enumerate(sizes) for j in range(size)]

    def columns(k, c):
        return pl.ds(pl.multiple_of(place_ref[k * NX + c] * width, width), width)

    def fetch(k, c):
        return pltpu.make_async_copy(
            tokens_ref.at[:, columns(k, c)],
            token_buf.at[k, :, pl.ds(c * width, width)],
            in_sem.at[k, c],
        )

    def put(k, c):
        return pltpu.make_async_copy(
            grad_buf.at[k, :, pl.ds(c * width, width)],
            grad_out.at[:, columns(k, c)],
            out_sem.at[k, c],
        )

    for k in range(len(pieces)):
        for c in range(NX):
            fetch(k, c).start()
    grads = grads_ref[...]
    total = None if first else sum_ref[...]
    for k, (i, j) in enumerate(pieces):
        weight = weight_refs[i][pl.ds(j * NX * width, NX * width), :]
        grad_buf[k] = lax.dot_general(
            grads, weight, (((1,), (1,)), ((), ())), preferred_element_type=F32
        ).astype(BF16)
        for c in range(NX):
            put(k, c).start()
        for c in range(NX):
            fetch(k, c).wait()
        term = jnp.dot(token_buf[k], weight, preferred_element_type=F32)
        total = term if total is None else total + term
    sum_out[...] = total.astype(sum_out.dtype)
    for k in range(len(pieces)):
        for c in range(NX):
            put(k, c).wait()


def project(tokens, grads, weights, place, state, last, span=1):
    rows, heads = grads.shape
    tokens = pltpu.with_memory_space_constraint(tokens, pltpu.HBM)
    width = tokens.shape[1] // (NY * NX * NZ)
    pair = NX * width
    sizes = tuple(w.shape[0] // pair for w in weights)
    count = sum(sizes)
    first = state is None
    whole = pl.BlockSpec(memory_space=pltpu.VMEM)
    n_in = 3 + len(weights)
    return pl.pallas_call(
        functools.partial(project_kernel, sizes, first, last),
        in_specs=[pl.BlockSpec(memory_space=pltpu.SMEM), HBM, whole]
        + [whole] * len(weights)
        + ([] if first else [whole, HBM]),
        out_specs=(whole, HBM),
        out_shape=(
            jax.ShapeDtypeStruct((rows, heads), BF16 if last else F32),
            pltpu.HBM(tokens.shape, BF16),
        ),
        scratch_shapes=[
            pltpu.VMEM((count, rows, pair), BF16),
            pltpu.VMEM((count, rows, pair), BF16),
            pltpu.SemaphoreType.DMA((count, NX)),
            pltpu.SemaphoreType.DMA((count, NX)),
        ],
        input_output_aliases={} if first else {n_in + 1: 1},
        compiler_params=pltpu.CompilerParams(vmem_limit_bytes=24 << 20),
        cost_estimate=pl.CostEstimate(
            flops=span * 4 * rows * heads * count * pair,
            bytes_accessed=count * pair * (rows * 4 + heads * 2),
            transcendentals=0,
        ),
        name="project",
    )(place, tokens, grads, *weights, *(() if first else state))


def outer_kernel(plan_ref, rank_ref, near_ref, far_ref, inner_ref, *refs):
    states, (new_ref, mom_ref) = refs[:-2], refs[-2:]
    groups, width = len(states), mom_ref.shape[1]
    rank = rank_ref[0]
    for b in range(groups):
        head = b ^ rank
        columns = pl.ds(pl.multiple_of(head * width, width), width)
        anchor, momentum = states[b][0], states[b][1]
        mean = (near_ref[:, columns] + far_ref[:, columns]) / groups
        pseudo = anchor - mean
        following = momentum_coef * momentum + pseudo
        outer = anchor - outer_rate * (pseudo + momentum_coef * following)
        synced = jnp.full(outer.shape, plan_ref[head], jnp.int32) > 0
        new_ref[:, columns] = jnp.where(synced, outer, inner_ref[:, columns]).astype(BF16)
        if b == 0:
            mom_ref[...] = jnp.where(synced, following, momentum)


def outer_step(plan, rank, near, far, inner, state):
    smem = pl.BlockSpec(memory_space=pltpu.SMEM)
    whole = pl.BlockSpec(memory_space=pltpu.VMEM)
    return pl.pallas_call(
        outer_kernel,
        in_specs=[smem, smem] + [whole] * (3 + len(state)),
        out_specs=(whole, whole),
        out_shape=(
            jax.ShapeDtypeStruct(inner.shape, BF16),
            jax.ShapeDtypeStruct(state[0].shape[1:], F32),
        ),
        name="outer_step",
    )(plan, rank, near, far, inner, *state)


def local(acts, out_grad, weights, anchor, momentum, plan):
    tokens, grads_out, local_weight = acts[0], out_grad[0], weights[0]
    rows, depth = tokens.shape
    heads = grads_out.shape[1]
    total_tokens = rows * NY * NX * NZ
    inner_rate = 1.0 / math.sqrt(total_tokens * depth)
    z = lax.axis_index("z")
    rank = lax.axis_index(REP)
    part = depth // SUB
    sub = ("y", "xl")

    width = part // NZ
    after = lambda x, *others: lax.optimization_barrier((x, *others))[0]

    width = part // NZ
    after = lambda x, *others: lax.optimization_barrier((x, *others))[0]

    pair = jnp.stack([local_weight, shift_x(local_weight)])
    block = jnp.stack([pair] + [shift_y(pair, dy) for dy in range(1, NY)])
    block = block.reshape(part, heads)

    place = jnp.stack([(z + d) % NZ for d in range(NZ)]).astype(jnp.int32)
    first, second = sort_tokens(tokens, grads_out, place)
    block, first = lax.optimization_barrier((block, first))
    first = lax.all_to_all(first, sub, 0, 0)

    y, x = lax.axis_index("y"), lax.axis_index("xl")

    def places(*shifts, rows=range(NY)):
        members = [(y - v) % NY * NX + (x ^ c) for v in rows for c in range(NX)]
        at = [member * NZ + (z + dz) % NZ for dz in shifts for member in members]
        return jnp.stack(at).astype(jnp.int32)

    carries = [project(tokens, grads_out, [block], places(0), None, False)]
    ring = [(block, block)]

    def ring_step(k, span, *earlier):
        right, left = ring[-1]
        if earlier:
            right, left = after(right, *earlier), after(left, *earlier)
        ring.append((shift_z(right, 1), shift_z(left, -1)))
        carries.append(
            project(tokens, grads_out, list(ring[-1]), places(-k, k), carries[-1], False, span)
        )

    ring_step(1, 5)
    ring_step(2, 1)

    first, _ = lax.optimization_barrier((first, carries[1][0]))
    second = lax.all_to_all(after(second, first), sub, 0, 0)
    state = after(jnp.stack([anchor, momentum]), first)
    first, ring[2] = lax.optimization_barrier((first, ring[2]))
    terms = {}
    for s, stage in enumerate(STAGES):
        if s == 1:
            second = after(second, carries[2][0])
        sums = partial_grad((first, second)[s], first, heads, width, s == 0)
        terms.update({d: sums[i] for i, d in enumerate(stage)})

    half = width // 2
    right = shift_z(terms[4][:half], 1)
    left = shift_z(terms[4][half:], -1)
    right = jnp.concatenate([terms[3][:half] + right, terms[3][half:]])
    left = jnp.concatenate([terms[5][:half], terms[5][half:] + left])
    right, left = shift_z(right, 1), shift_z(left, -1)
    ring_step(3, 1, right, left)
    states = [state, shift_core(state)]
    right, left = terms[2] + right, terms[6] + left
    right, left, states = lax.optimization_barrier((right, left, states))
    right, left = shift_z(right, 1), shift_z(left, -1)
    states += [shift_far(x) for x in states]
    right, left = terms[1] + right, terms[7] + left
    right, left, states, ring[3] = lax.optimization_barrier((right, left, states, ring[3]))
    right, left = shift_z(right, 1), shift_z(left, -1)
    right = after(right, carries[3][0])
    inner = local_weight.astype(F32) - inner_rate * (terms[0] + right + left)

    near = inner + shift_core(inner)
    half = part // 2
    right, left = shift_z(ring[3][0][:half], 1), shift_z(ring[3][1][half:], -1)
    near, right, left = lax.optimization_barrier((near, right, left))
    far = shift_far(near)
    values, act_grad = project(tokens, grads_out, [right, left], places(4), carries[3], True)
    new_weight, new_momentum = outer_step(
        plan, jnp.reshape(rank, (1,)).astype(jnp.int32), near, far, inner, states
    )
    return values[None], act_grad[None], new_weight[None], new_momentum


def solution(mesh):
    fine = Mesh(mesh.devices.reshape(2, 2, NY, NX, NZ), ("xh", "core", "y", "xl", "z"))
    placed = (
        P(REP, FSDP, None),
        P(REP, FSDP, None),
        P(REP, FSDP, None),
        P(FSDP, REP),
        P(FSDP, REP),
        P(),
    )
    return jax.shard_map(
        local,
        mesh=fine,
        in_specs=placed,
        out_specs=(
            P(REP, FSDP, None),
            P(REP, FSDP, None),
            P(REP, FSDP, None),
            P(FSDP, REP),
        ),
        check_vma=False,
    )
```

```python
import functools
import math

import jax
import jax.numpy as jnp
from jax import lax
from jax.experimental import pallas as pl
from jax.experimental.pallas import tpu as pltpu
from jax.sharding import Mesh, PartitionSpec as P

outer_rate = 0.7
momentum_coef = 0.9
NY, NX, NZ = 4, 2, 8
SUB = NY * NX
REP = ("xh", "core")
FSDP = ("y", "xl", "z")
HBM = pl.BlockSpec(memory_space=pltpu.HBM)
F32 = jnp.float32
BF16 = jnp.bfloat16
STAGES = ((4, 3, 5), (2, 6, 1, 7, 0))


def shift_z(x, dz):
    return lax.ppermute(x, "z", [(i, (i + dz) % NZ) for i in range(NZ)])


def shift_y(x, dy):
    return lax.ppermute(x, "y", [(i, (i + dy) % NY) for i in range(NY)])


def shift_x(x):
    return lax.ppermute(x, "xl", [(0, 1), (1, 0)])


def shift_core(x):
    return lax.ppermute(x, "core", [(0, 1), (1, 0)])


def shift_far(x):
    return lax.ppermute(x, "xh", [(0, 1), (1, 0)])


def sort_kernel(place_ref, tokens_ref, grads_ref, *refs):
    n = len(STAGES)
    outs, (tokens_buf, grads_buf), bufs, (in_sem, out_sem) = (
        refs[:n], refs[n : n + 2], refs[n + 2 : 2 * n + 2], refs[2 * n + 2 :]
    )
    heads = grads_ref.shape[1]
    part = tokens_buf.shape[2]
    width = part // NZ
    fetches = [pltpu.make_async_copy(grads_ref, grads_buf, in_sem.at[SUB])]
    for j in range(SUB):
        fetches.append(
            pltpu.make_async_copy(
                tokens_ref.at[:, pl.ds(j * part, part)], tokens_buf.at[j], in_sem.at[j]
            )
        )
    for fetch in fetches:
        fetch.start()
    fetches[0].wait()
    puts = []
    for j in range(SUB):
        fetches[1 + j].wait()
        bufs[0][j, :, :heads] = grads_buf[...]
        for s, stage in enumerate(STAGES):
            start = heads if s == 0 else 0
            for i, d in enumerate(stage):
                source = pl.multiple_of(place_ref[d] * width, width)
                bufs[s][j, :, pl.ds(start + i * width, width)] = tokens_buf[
                    j, :, pl.ds(source, width)
                ]
            put = pltpu.make_async_copy(bufs[s].at[j], outs[s].at[j], out_sem.at[s, j])
            put.start()
            puts.append(put)
    for put in puts:
        put.wait()


def sort_tokens(tokens, grads, place):
    tokens = pltpu.with_memory_space_constraint(tokens, pltpu.HBM)
    grads = pltpu.with_memory_space_constraint(grads, pltpu.HBM)
    rows, depth = tokens.shape
    heads = grads.shape[1]
    part = depth // SUB
    width = part // NZ
    sizes = [len(stage) * width + (heads if s == 0 else 0) for s, stage in enumerate(STAGES)]
    return pl.pallas_call(
        sort_kernel,
        in_specs=[pl.BlockSpec(memory_space=pltpu.SMEM), HBM, HBM],
        out_specs=(HBM,) * len(sizes),
        out_shape=tuple(pltpu.HBM((SUB, rows, n), tokens.dtype) for n in sizes),
        scratch_shapes=[
            pltpu.VMEM((SUB, rows, part), tokens.dtype),
            pltpu.VMEM((rows, heads), tokens.dtype),
            *[pltpu.VMEM((SUB, rows, n), tokens.dtype) for n in sizes],
            pltpu.SemaphoreType.DMA((SUB + 1,)),
            pltpu.SemaphoreType.DMA((len(sizes), SUB)),
        ],
        compiler_params=pltpu.CompilerParams(vmem_limit_bytes=14 << 20),
        cost_estimate=pl.CostEstimate(
            flops=0, bytes_accessed=4 * rows * (depth + heads), transcendentals=0
        ),
        name="sort_tokens",
    )(place, tokens, grads)


def grad_kernel(tokens_ref, grads_ref, out_ref):
    members, rows, width = tokens_ref.shape
    heads = grads_ref.shape[2]
    out_ref[0] = lax.dot_general(
        tokens_ref[...].reshape(members * rows, width),
        grads_ref[...].reshape(members * rows, heads),
        (((0,), (0,)), ((), ())),
        preferred_element_type=F32,
    )


def partial_grad(tokens, first, heads, width, at, count, span):
    members, rows, _ = tokens.shape
    return pl.pallas_call(
        grad_kernel,
        grid=(count,),
        in_specs=[
            pl.BlockSpec((members, rows, width), lambda d: (0, 0, d + at)),
            pl.BlockSpec((members, rows, heads), lambda d: (0, 0, 0)),
        ],
        out_specs=pl.BlockSpec((1, width, heads), lambda d: (d, 0, 0)),
        out_shape=jax.ShapeDtypeStruct((count, width, heads), F32),
        compiler_params=pltpu.CompilerParams(vmem_limit_bytes=10 << 20),
        cost_estimate=pl.CostEstimate(
            flops=span * 2 * members * rows * count * width * heads,
            bytes_accessed=0,
            transcendentals=0,
        ),
        name="partial_grad",
    )(tokens, first)


def project_kernel(sizes, first, place_ref, tokens_ref, grads_ref, *refs):
    n = len(sizes)
    weight_refs, refs = refs[:n], refs[n:]
    if not first:
        sum_ref, _, refs = refs[0], refs[1], refs[2:]
    sum_out, grad_out, token_buf, grad_buf, in_sem, out_sem = refs
    count = sum(sizes)
    width = token_buf.shape[1] // count

    def columns(k):
        return pl.ds(pl.multiple_of(place_ref[k] * width, width), width)

    def fetch(k):
        return pltpu.make_async_copy(
            tokens_ref.at[:, columns(k)], token_buf.at[:, pl.ds(k * width, width)], in_sem.at[k]
        )

    def put(k):
        return pltpu.make_async_copy(
            grad_buf.at[:, pl.ds(k * width, width)], grad_out.at[:, columns(k)], out_sem.at[k]
        )

    for k in range(count):
        fetch(k).start()
    grads = grads_ref[...]
    at = 0
    for weight_ref, size in zip(weight_refs, sizes):
        for j in range(0, size, 4):
            grad_buf[:, pl.ds((at + j) * width, 4 * width)] = lax.dot_general(
                grads,
                weight_ref[pl.ds(j * width, 4 * width), :],
                (((1,), (1,)), ((), ())),
                preferred_element_type=F32,
            ).astype(BF16)
            for k in range(at + j, at + j + 4):
                put(k).start()
        at += size
    for k in range(count):
        fetch(k).wait()
    total, at = None if first else sum_ref[...], 0
    for weight_ref, size in zip(weight_refs, sizes):
        term = jnp.dot(
            token_buf[:, pl.ds(at * width, size * width)],
            weight_ref[...],
            preferred_element_type=F32,
        )
        total = term if total is None else total + term
        at += size
    sum_out[...] = total.astype(sum_out.dtype)
    for k in range(count):
        put(k).wait()


def project(tokens, grads, weights, place, state, last, span=1):
    rows, heads = grads.shape
    tokens = pltpu.with_memory_space_constraint(tokens, pltpu.HBM)
    width = tokens.shape[1] // (NY * NX * NZ)
    sizes = tuple(w.shape[0] // width for w in weights)
    count = sum(sizes)
    first = state is None
    whole = pl.BlockSpec(memory_space=pltpu.VMEM)
    n_in = 3 + len(weights)
    return pl.pallas_call(
        functools.partial(project_kernel, sizes, first),
        in_specs=[pl.BlockSpec(memory_space=pltpu.SMEM), HBM, whole]
        + [whole] * len(weights)
        + ([] if first else [whole, HBM]),
        out_specs=(whole, HBM),
        out_shape=(
            jax.ShapeDtypeStruct((rows, heads), BF16 if last else F32),
            pltpu.HBM(tokens.shape, BF16),
        ),
        scratch_shapes=[
            pltpu.VMEM((rows, count * width), BF16),
            pltpu.VMEM((rows, count * width), BF16),
            pltpu.SemaphoreType.DMA((count,)),
            pltpu.SemaphoreType.DMA((count,)),
        ],
        input_output_aliases={} if first else {n_in + 1: 1},
        compiler_params=pltpu.CompilerParams(vmem_limit_bytes=14 << 20),
        cost_estimate=pl.CostEstimate(
            flops=span * 4 * rows * heads * count * width,
            bytes_accessed=count * width * (rows * 4 + heads * 2),
            transcendentals=0,
        ),
        name="project",
    )(place, tokens, grads, *weights, *(() if first else state))


def outer_kernel(plan_ref, rank_ref, near_ref, far_ref, inner_ref, *refs):
    states, (new_ref, mom_ref) = refs[:-2], refs[-2:]
    groups, width = len(states), mom_ref.shape[1]
    rank = rank_ref[0]
    for b in range(groups):
        head = b ^ rank
        columns = pl.ds(pl.multiple_of(head * width, width), width)
        anchor, momentum = states[b][0], states[b][1]
        mean = (near_ref[:, columns] + far_ref[:, columns]) / groups
        pseudo = anchor - mean
        following = momentum_coef * momentum + pseudo
        outer = anchor - outer_rate * (pseudo + momentum_coef * following)
        synced = jnp.full(outer.shape, plan_ref[head], jnp.int32) > 0
        new_ref[:, columns] = jnp.where(synced, outer, inner_ref[:, columns]).astype(BF16)
        if b == 0:
            mom_ref[...] = jnp.where(synced, following, momentum)


def outer_step(plan, rank, near, far, inner, state):
    smem = pl.BlockSpec(memory_space=pltpu.SMEM)
    whole = pl.BlockSpec(memory_space=pltpu.VMEM)
    return pl.pallas_call(
        outer_kernel,
        in_specs=[smem, smem] + [whole] * (3 + len(state)),
        out_specs=(whole, whole),
        out_shape=(
            jax.ShapeDtypeStruct(inner.shape, BF16),
            jax.ShapeDtypeStruct(state[0].shape[1:], F32),
        ),
        compiler_params=pltpu.CompilerParams(vmem_limit_bytes=4 << 20),
        name="outer_step",
    )(plan, rank, near, far, inner, *state)


def local(acts, out_grad, weights, anchor, momentum, plan):
    tokens, grads_out, local_weight = acts[0], out_grad[0], weights[0]
    rows, depth = tokens.shape
    heads = grads_out.shape[1]
    total_tokens = rows * NY * NX * NZ
    inner_rate = 1.0 / math.sqrt(total_tokens * depth)
    z = lax.axis_index("z")
    rank = lax.axis_index(REP)
    part = depth // SUB
    sub = ("y", "xl")

    width = part // NZ
    after = lambda x, *others: lax.optimization_barrier((x, *others))[0]

    width = part // NZ
    after = lambda x, *others: lax.optimization_barrier((x, *others))[0]

    pair = jnp.stack([local_weight, shift_x(local_weight)])
    block = jnp.stack([pair] + [shift_y(pair, dy) for dy in range(1, NY)])
    block = block.reshape(part, heads)

    place = jnp.stack([(z + d) % NZ for d in range(NZ)]).astype(jnp.int32)
    first, second = sort_tokens(tokens, grads_out, place)
    block, first = lax.optimization_barrier((block, first))
    first = lax.all_to_all(first, sub, 0, 0)

    y, x = lax.axis_index("y"), lax.axis_index("xl")

    def places(*shifts):
        members = [(y - v) % NY * NX + (x ^ c) for v in range(NY) for c in range(NX)]
        at = [member * NZ + (z + dz) % NZ for dz in shifts for member in members]
        return jnp.stack(at).astype(jnp.int32)

    carries = [project(tokens, grads_out, [block], places(0), None, False)]
    ring = [(block, block)]

    def ring_step(k, span, *earlier):
        right, left = ring[-1]
        if earlier:
            right, left = after(right, *earlier), after(left, *earlier)
        ring.append((shift_z(right, 1), shift_z(left, -1)))
        at = places(-k, k)
        carries.append(
            project(tokens, grads_out, list(ring[-1]), at, carries[-1], False, span)
        )

    ring_step(1, 5)
    ring_step(2, 5)

    first, _ = lax.optimization_barrier((first, carries[1][0]))
    second = lax.all_to_all(after(second, first), sub, 0, 0)
    state = after(jnp.stack([anchor, momentum]), first)
    first, ring[2] = lax.optimization_barrier((first, ring[2]))
    def terms(*distances):
        s = 0 if distances[0] in STAGES[0] else 1
        at = STAGES[s].index(distances[0]) + (heads // width if s == 0 else 0)
        span = 8 if s == 0 else 1
        return partial_grad((first, second)[s], first, heads, width, at, len(distances), span)

    half = width // 2
    middle, ahead, back = terms(4, 3, 5)
    right, left = shift_z(middle[:half], 1), shift_z(middle[half:], -1)
    states = [state, shift_core(state)]
    right = jnp.concatenate([ahead[:half] + right, ahead[half:]])
    left = jnp.concatenate([back[:half], back[half:] + left])
    right, left, states = lax.optimization_barrier((right, left, states))
    right, left = shift_z(right, 1), shift_z(left, -1)
    ring_step(3, 1, right, left)
    ahead, back = terms(2, 6)
    right, left = ahead + right, back + left
    states += [shift_far(x) for x in states]
    right, left = shift_z(right, 1), shift_z(left, -1)
    second, states, _ = lax.optimization_barrier((second, states, carries[2][0]))
    ahead, back, rest = terms(1, 7, 0)
    right, left = ahead + right, back + left
    right, left, ring[3] = lax.optimization_barrier((right, left, ring[3]))
    right, left = shift_z(right, 1), shift_z(left, -1)
    inner = local_weight.astype(F32) - inner_rate * (rest + right + left)

    near = inner + shift_core(inner)
    far = shift_far(near)
    half = part // 2
    right, left = shift_z(ring[3][0][:half], 1), shift_z(ring[3][1][half:], -1)
    values, act_grad = project(tokens, grads_out, [right, left], places(4), carries[3], True)
    new_weight, new_momentum = outer_step(
        plan, jnp.reshape(rank, (1,)).astype(jnp.int32), near, far, inner, states
    )
    return values[None], act_grad[None], new_weight[None], new_momentum


def solution(mesh):
    fine = Mesh(mesh.devices.reshape(2, 2, NY, NX, NZ), ("xh", "core", "y", "xl", "z"))
    placed = (
        P(REP, FSDP, None),
        P(REP, FSDP, None),
        P(REP, FSDP, None),
        P(FSDP, REP),
        P(FSDP, REP),
        P(),
    )
    return jax.shard_map(
        local,
        mesh=fine,
        in_specs=placed,
        out_specs=(
            P(REP, FSDP, None),
            P(REP, FSDP, None),
            P(REP, FSDP, None),
            P(FSDP, REP),
        ),
        check_vma=False,
    )
```

```python
import functools
import math

import jax
import jax.numpy as jnp
from jax import lax
from jax.experimental import pallas as pl
from jax.experimental.pallas import tpu as pltpu
from jax.sharding import Mesh, PartitionSpec as P

outer_rate = 0.7
momentum_coef = 0.9
NY, NX, NZ = 4, 2, 8
SUB = NY * NX
REP = ("xh", "core")
FSDP = ("y", "xl", "z")
HBM = pl.BlockSpec(memory_space=pltpu.HBM)
F32 = jnp.float32
BF16 = jnp.bfloat16
STAGES = ((4, 3, 5), (2, 6, 1, 7, 0))


def shift_z(x, dz):
    return lax.ppermute(x, "z", [(i, (i + dz) % NZ) for i in range(NZ)])


def shift_y(x, dy):
    return lax.ppermute(x, "y", [(i, (i + dy) % NY) for i in range(NY)])


def shift_x(x):
    return lax.ppermute(x, "xl", [(0, 1), (1, 0)])


def shift_core(x):
    return lax.ppermute(x, "core", [(0, 1), (1, 0)])


def shift_far(x):
    return lax.ppermute(x, "xh", [(0, 1), (1, 0)])


def sort_kernel(place_ref, tokens_ref, grads_ref, *refs):
    n = len(STAGES)
    outs, (tokens_buf, grads_buf), bufs, (in_sem, out_sem) = (
        refs[:n], refs[n : n + 2], refs[n + 2 : 2 * n + 2], refs[2 * n + 2 :]
    )
    heads = grads_ref.shape[1]
    part = tokens_buf.shape[2]
    width = part // NZ
    fetches = [pltpu.make_async_copy(grads_ref, grads_buf, in_sem.at[SUB])]
    for j in range(SUB):
        fetches.append(
            pltpu.make_async_copy(
                tokens_ref.at[:, pl.ds(j * part, part)], tokens_buf.at[j], in_sem.at[j]
            )
        )
    for fetch in fetches:
        fetch.start()
    fetches[0].wait()
    puts = []
    for j in range(SUB):
        fetches[1 + j].wait()
        bufs[0][j, :, :heads] = grads_buf[...]
        for s, stage in enumerate(STAGES):
            start = heads if s == 0 else 0
            for i, d in enumerate(stage):
                source = pl.multiple_of(place_ref[d] * width, width)
                bufs[s][j, :, pl.ds(start + i * width, width)] = tokens_buf[
                    j, :, pl.ds(source, width)
                ]
            put = pltpu.make_async_copy(bufs[s].at[j], outs[s].at[j], out_sem.at[s, j])
            put.start()
            puts.append(put)
    for put in puts:
        put.wait()


def sort_tokens(tokens, grads, place):
    tokens = pltpu.with_memory_space_constraint(tokens, pltpu.HBM)
    grads = pltpu.with_memory_space_constraint(grads, pltpu.HBM)
    rows, depth = tokens.shape
    heads = grads.shape[1]
    part = depth // SUB
    width = part // NZ
    sizes = [len(stage) * width + (heads if s == 0 else 0) for s, stage in enumerate(STAGES)]
    return pl.pallas_call(
        sort_kernel,
        in_specs=[pl.BlockSpec(memory_space=pltpu.SMEM), HBM, HBM],
        out_specs=(HBM,) * len(sizes),
        out_shape=tuple(pltpu.HBM((SUB, rows, n), tokens.dtype) for n in sizes),
        scratch_shapes=[
            pltpu.VMEM((SUB, rows, part), tokens.dtype),
            pltpu.VMEM((rows, heads), tokens.dtype),
            *[pltpu.VMEM((SUB, rows, n), tokens.dtype) for n in sizes],
            pltpu.SemaphoreType.DMA((SUB + 1,)),
            pltpu.SemaphoreType.DMA((len(sizes), SUB)),
        ],
        compiler_params=pltpu.CompilerParams(vmem_limit_bytes=14 << 20),
        cost_estimate=pl.CostEstimate(
            flops=0, bytes_accessed=8 * rows * (depth + heads), transcendentals=0
        ),
        name="sort_tokens",
    )(place, tokens, grads)


def grad_kernel(tokens_ref, grads_ref, out_ref):
    members, rows, width = tokens_ref.shape
    heads = grads_ref.shape[2]
    out_ref[0] = lax.dot_general(
        tokens_ref[...].reshape(members * rows, width),
        grads_ref[...].reshape(members * rows, heads),
        (((0,), (0,)), ((), ())),
        preferred_element_type=F32,
    )


def partial_grad(tokens, first, heads, width, at, count, span):
    members, rows, _ = tokens.shape
    return pl.pallas_call(
        grad_kernel,
        grid=(count,),
        in_specs=[
            pl.BlockSpec((members, rows, width), lambda d: (0, 0, d + at)),
            pl.BlockSpec((members, rows, heads), lambda d: (0, 0, 0)),
        ],
        out_specs=pl.BlockSpec((1, width, heads), lambda d: (d, 0, 0)),
        out_shape=jax.ShapeDtypeStruct((count, width, heads), F32),
        compiler_params=pltpu.CompilerParams(vmem_limit_bytes=10 << 20),
        cost_estimate=pl.CostEstimate(
            flops=span * 2 * members * rows * count * width * heads,
            bytes_accessed=0,
            transcendentals=0,
        ),
        name="partial_grad",
    )(tokens, first)


def project_kernel(sizes, first, place_ref, tokens_ref, grads_ref, *refs):
    n = len(sizes)
    weight_refs, refs = refs[:n], refs[n:]
    if not first:
        sum_ref, _, refs = refs[0], refs[1], refs[2:]
    sum_out, grad_out, token_buf, grad_buf, in_sem, out_sem = refs
    count = sum(sizes)
    width = token_buf.shape[1] // count

    def columns(k):
        return pl.ds(pl.multiple_of(place_ref[k] * width, width), width)

    def fetch(k):
        return pltpu.make_async_copy(
            tokens_ref.at[:, columns(k)], token_buf.at[:, pl.ds(k * width, width)], in_sem.at[k]
        )

    def put(k):
        return pltpu.make_async_copy(
            grad_buf.at[:, pl.ds(k * width, width)], grad_out.at[:, columns(k)], out_sem.at[k]
        )

    for k in range(count):
        fetch(k).start()
    grads = grads_ref[...]
    at = 0
    for weight_ref, size in zip(weight_refs, sizes):
        for j in range(0, size, 4):
            grad_buf[:, pl.ds((at + j) * width, 4 * width)] = lax.dot_general(
                grads,
                weight_ref[pl.ds(j * width, 4 * width), :],
                (((1,), (1,)), ((), ())),
                preferred_element_type=F32,
            ).astype(BF16)
            for k in range(at + j, at + j + 4):
                put(k).start()
        at += size
    for k in range(count):
        fetch(k).wait()
    total, at = None if first else sum_ref[...], 0
    for weight_ref, size in zip(weight_refs, sizes):
        term = jnp.dot(
            token_buf[:, pl.ds(at * width, size * width)],
            weight_ref[...],
            preferred_element_type=F32,
        )
        total = term if total is None else total + term
        at += size
    sum_out[...] = total.astype(sum_out.dtype)
    for k in range(count):
        put(k).wait()


def project(tokens, grads, weights, place, state, last, span=1):
    rows, heads = grads.shape
    tokens = pltpu.with_memory_space_constraint(tokens, pltpu.HBM)
    width = tokens.shape[1] // (NY * NX * NZ)
    sizes = tuple(w.shape[0] // width for w in weights)
    count = sum(sizes)
    first = state is None
    whole = pl.BlockSpec(memory_space=pltpu.VMEM)
    n_in = 3 + len(weights)
    return pl.pallas_call(
        functools.partial(project_kernel, sizes, first),
        in_specs=[pl.BlockSpec(memory_space=pltpu.SMEM), HBM, whole]
        + [whole] * len(weights)
        + ([] if first else [whole, HBM]),
        out_specs=(whole, HBM),
        out_shape=(
            jax.ShapeDtypeStruct((rows, heads), BF16 if last else F32),
            pltpu.HBM(tokens.shape, BF16),
        ),
        scratch_shapes=[
            pltpu.VMEM((rows, count * width), BF16),
            pltpu.VMEM((rows, count * width), BF16),
            pltpu.SemaphoreType.DMA((count,)),
            pltpu.SemaphoreType.DMA((count,)),
        ],
        input_output_aliases={} if first else {n_in + 1: 1},
        compiler_params=pltpu.CompilerParams(vmem_limit_bytes=14 << 20),
        cost_estimate=pl.CostEstimate(
            flops=span * 4 * rows * heads * count * width,
            bytes_accessed=count * width * (rows * 4 + heads * 2),
            transcendentals=0,
        ),
        name="project",
    )(place, tokens, grads, *weights, *(() if first else state))


def outer_kernel(plan_ref, rank_ref, near_ref, far_ref, inner_ref, *refs):
    states, (new_ref, mom_ref) = refs[:-2], refs[-2:]
    groups, width = len(states), mom_ref.shape[1]
    rank = rank_ref[0]
    for b in range(groups):
        head = b ^ rank
        columns = pl.ds(pl.multiple_of(head * width, width), width)
        anchor, momentum = states[b][0], states[b][1]
        mean = (near_ref[:, columns] + far_ref[:, columns]) / groups
        pseudo = anchor - mean
        following = momentum_coef * momentum + pseudo
        outer = anchor - outer_rate * (pseudo + momentum_coef * following)
        synced = jnp.full(outer.shape, plan_ref[head], jnp.int32) > 0
        new_ref[:, columns] = jnp.where(synced, outer, inner_ref[:, columns]).astype(BF16)
        if b == 0:
            mom_ref[...] = jnp.where(synced, following, momentum)


def outer_step(plan, rank, near, far, inner, state):
    smem = pl.BlockSpec(memory_space=pltpu.SMEM)
    whole = pl.BlockSpec(memory_space=pltpu.VMEM)
    return pl.pallas_call(
        outer_kernel,
        in_specs=[smem, smem] + [whole] * (3 + len(state)),
        out_specs=(whole, whole),
        out_shape=(
            jax.ShapeDtypeStruct(inner.shape, BF16),
            jax.ShapeDtypeStruct(state[0].shape[1:], F32),
        ),
        compiler_params=pltpu.CompilerParams(vmem_limit_bytes=4 << 20),
        name="outer_step",
    )(plan, rank, near, far, inner, *state)


def local(acts, out_grad, weights, anchor, momentum, plan):
    tokens, grads_out, local_weight = acts[0], out_grad[0], weights[0]
    rows, depth = tokens.shape
    heads = grads_out.shape[1]
    total_tokens = rows * NY * NX * NZ
    inner_rate = 1.0 / math.sqrt(total_tokens * depth)
    z = lax.axis_index("z")
    rank = lax.axis_index(REP)
    part = depth // SUB
    sub = ("y", "xl")

    width = part // NZ
    after = lambda x, *others: lax.optimization_barrier((x, *others))[0]

    width = part // NZ
    after = lambda x, *others: lax.optimization_barrier((x, *others))[0]

    beside = shift_x(local_weight)
    moved = [local_weight, beside]
    for dy in range(1, NY):
        moved += [shift_y(local_weight, dy), shift_y(beside, dy)]
    block = [jnp.concatenate(moved[:NY]), jnp.concatenate(moved[NY:])]

    place = jnp.stack([(z + d) % NZ for d in range(NZ)]).astype(jnp.int32)
    first, second = sort_tokens(tokens, grads_out, place)
    block, first = lax.optimization_barrier((block, first))
    first = lax.all_to_all(first, sub, 0, 0)

    y, x = lax.axis_index("y"), lax.axis_index("xl")

    def places(*shifts):
        members = [(y - v) % NY * NX + (x ^ c) for v in range(NY) for c in range(NX)]
        at = [member * NZ + (z + dz) % NZ for dz in shifts for member in members]
        return jnp.stack(at).astype(jnp.int32)

    def add(carry, k, pieces, span=1, last=False):
        at = places(k) if k in (0, 4) else places(-k, k)
        return project(tokens, grads_out, pieces, at, carry, last, span)

    right, left = (
        [[block[h]] for h in range(2)],
        [[block[h]] for h in range(2)],
    )
    carry = add(None, 0, block)
    for k in (1, 2):
        for h in range(2):
            right[h].append(shift_z(right[h][-1], 1))
            left[h].append(shift_z(left[h][-1], -1))
    carry = add(carry, 1, [right[0][1], right[1][1], left[0][1], left[1][1]], 10)

    first, _ = lax.optimization_barrier((first, carry[0]))
    second = lax.all_to_all(after(second, first), sub, 0, 0)
    state = after(jnp.stack([anchor, momentum]), first)
    step2 = [right[0][2], right[1][2], left[0][2], left[1][2]]
    first, step2 = lax.optimization_barrier((first, step2))
    carry = add(carry, 2, step2, 3)

    def terms(*distances):
        s = 0 if distances[0] in STAGES[0] else 1
        at = STAGES[s].index(distances[0]) + (heads // width if s == 0 else 0)
        span = 13 if s == 0 else 1
        return partial_grad((first, second)[s], first, heads, width, at, len(distances), span)

    half = width // 2
    middle, ahead, back = terms(4, 3, 5)
    up, down = shift_z(middle[:half], 1), shift_z(middle[half:], -1)
    states = [state, shift_core(state)]
    up = jnp.concatenate([ahead[:half] + up, ahead[half:]])
    down = jnp.concatenate([back[:half], back[half:] + down])
    up, down, states = lax.optimization_barrier((up, down, states))
    up, down = shift_z(up, 1), shift_z(down, -1)
    step3 = [None] * 4
    step3[0] = shift_z(after(step2[0], up, down), 1)
    step3[3] = shift_z(after(step2[3], up, down), -1)
    ahead, back = terms(2, 6)
    up, down = ahead + up, back + down
    states += [shift_far(x) for x in states]
    up, down = shift_z(up, 1), shift_z(down, -1)
    second, states = lax.optimization_barrier((second, states))
    ahead, back, rest = terms(1, 7, 0)
    step3[1] = shift_z(after(step2[1], rest), 1)
    step3[2] = shift_z(after(step2[2], rest), -1)
    up, down = ahead + up, back + down
    up, down, step3[0], step3[3] = lax.optimization_barrier((up, down, step3[0], step3[3]))
    up, down = shift_z(up, 1), shift_z(down, -1)
    up, down, step3, _ = lax.optimization_barrier((up, down, step3, carry[0]))
    inner = local_weight.astype(F32) - inner_rate * (rest + up + down)

    near = inner + shift_core(inner)
    far = shift_far(near)
    step4 = [shift_z(step3[0], 1), shift_z(step3[3], -1)]
    carry = add(carry, 3, step3)
    values, act_grad = add(carry, 4, step4, last=True)
    new_weight, new_momentum = outer_step(
        plan, jnp.reshape(rank, (1,)).astype(jnp.int32), near, far, inner, states
    )
    return values[None], act_grad[None], new_weight[None], new_momentum


def solution(mesh):
    fine = Mesh(mesh.devices.reshape(2, 2, NY, NX, NZ), ("xh", "core", "y", "xl", "z"))
    placed = (
        P(REP, FSDP, None),
        P(REP, FSDP, None),
        P(REP, FSDP, None),
        P(FSDP, REP),
        P(FSDP, REP),
        P(),
    )
    return jax.shard_map(
        local,
        mesh=fine,
        in_specs=placed,
        out_specs=(
            P(REP, FSDP, None),
            P(REP, FSDP, None),
            P(REP, FSDP, None),
            P(FSDP, REP),
        ),
        check_vma=False,
    )
```

```python
import functools
import math

import jax
import jax.numpy as jnp
from jax import lax
from jax.experimental import pallas as pl
from jax.experimental.pallas import tpu as pltpu
from jax.sharding import Mesh, PartitionSpec as P

outer_rate = 0.7
momentum_coef = 0.9
NY, NX, NZ = 4, 2, 8
SUB = NY * NX
REP = ("xh", "core")
FSDP = ("y", "xl", "z")
HBM = pl.BlockSpec(memory_space=pltpu.HBM)
F32 = jnp.float32
BF16 = jnp.bfloat16
STAGES = ((4, 3, 5, 2, 6), (1, 7, 0))


def shift_z(x, dz):
    return lax.ppermute(x, "z", [(i, (i + dz) % NZ) for i in range(NZ)])


def shift_y(x, dy):
    return lax.ppermute(x, "y", [(i, (i + dy) % NY) for i in range(NY)])


def shift_x(x):
    return lax.ppermute(x, "xl", [(0, 1), (1, 0)])


def shift_core(x):
    return lax.ppermute(x, "core", [(0, 1), (1, 0)])


def shift_far(x):
    return lax.ppermute(x, "xh", [(0, 1), (1, 0)])


def sort_kernel(place_ref, tokens_ref, grads_ref, *refs):
    n = len(STAGES)
    outs, (tokens_buf, grads_buf), bufs, (in_sem, out_sem) = (
        refs[:n], refs[n : n + 2], refs[n + 2 : 2 * n + 2], refs[2 * n + 2 :]
    )
    heads = grads_ref.shape[1]
    part = tokens_buf.shape[2]
    width = part // NZ
    fetches = [pltpu.make_async_copy(grads_ref, grads_buf, in_sem.at[SUB])]
    for j in range(SUB):
        fetches.append(
            pltpu.make_async_copy(
                tokens_ref.at[:, pl.ds(j * part, part)], tokens_buf.at[j], in_sem.at[j]
            )
        )
    for fetch in fetches:
        fetch.start()
    fetches[0].wait()
    puts = []
    for j in range(SUB):
        fetches[1 + j].wait()
        bufs[0][j, :, :heads] = grads_buf[...]
        for s, stage in enumerate(STAGES):
            start = heads if s == 0 else 0
            for i, d in enumerate(stage):
                source = pl.multiple_of(place_ref[d] * width, width)
                bufs[s][j, :, pl.ds(start + i * width, width)] = tokens_buf[
                    j, :, pl.ds(source, width)
                ]
            put = pltpu.make_async_copy(bufs[s].at[j], outs[s].at[j], out_sem.at[s, j])
            put.start()
            puts.append(put)
    for put in puts:
        put.wait()


def sort_tokens(tokens, grads, place):
    tokens = pltpu.with_memory_space_constraint(tokens, pltpu.HBM)
    grads = pltpu.with_memory_space_constraint(grads, pltpu.HBM)
    rows, depth = tokens.shape
    heads = grads.shape[1]
    part = depth // SUB
    width = part // NZ
    sizes = [len(stage) * width + (heads if s == 0 else 0) for s, stage in enumerate(STAGES)]
    return pl.pallas_call(
        sort_kernel,
        in_specs=[pl.BlockSpec(memory_space=pltpu.SMEM), HBM, HBM],
        out_specs=(HBM,) * len(sizes),
        out_shape=tuple(pltpu.HBM((SUB, rows, n), tokens.dtype) for n in sizes),
        scratch_shapes=[
            pltpu.VMEM((SUB, rows, part), tokens.dtype),
            pltpu.VMEM((rows, heads), tokens.dtype),
            *[pltpu.VMEM((SUB, rows, n), tokens.dtype) for n in sizes],
            pltpu.SemaphoreType.DMA((SUB + 1,)),
            pltpu.SemaphoreType.DMA((len(sizes), SUB)),
        ],
        compiler_params=pltpu.CompilerParams(vmem_limit_bytes=12 << 20),
        cost_estimate=pl.CostEstimate(
            flops=0, bytes_accessed=8 * rows * (depth + heads), transcendentals=0
        ),
        name="sort_tokens",
    )(place, tokens, grads)


def grad_kernel(tokens_ref, grads_ref, out_ref):
    members, rows, width = tokens_ref.shape
    heads = grads_ref.shape[2]
    out_ref[0] = lax.dot_general(
        tokens_ref[...].reshape(members * rows, width),
        grads_ref[...].reshape(members * rows, heads),
        (((0,), (0,)), ((), ())),
        preferred_element_type=F32,
    )


def partial_grad(tokens, first, heads, width, at, count, span):
    members, rows, _ = tokens.shape
    return pl.pallas_call(
        grad_kernel,
        grid=(count,),
        in_specs=[
            pl.BlockSpec((members, rows, width), lambda d: (0, 0, d + at)),
            pl.BlockSpec((members, rows, heads), lambda d: (0, 0, 0)),
        ],
        out_specs=pl.BlockSpec((1, width, heads), lambda d: (d, 0, 0)),
        out_shape=jax.ShapeDtypeStruct((count, width, heads), F32),
        compiler_params=pltpu.CompilerParams(vmem_limit_bytes=8 << 20),
        cost_estimate=pl.CostEstimate(
            flops=span * 2 * members * rows * count * width * heads,
            bytes_accessed=0,
            transcendentals=0,
        ),
        name="partial_grad",
    )(tokens, first)


def project_kernel(sizes, first, place_ref, tokens_ref, grads_ref, *refs):
    n = len(sizes)
    weight_refs, refs = refs[:n], refs[n:]
    if not first:
        sum_ref, _, refs = refs[0], refs[1], refs[2:]
    sum_out, grad_out, token_buf, grad_buf, in_sem, out_sem = refs
    count = sum(sizes)
    width = token_buf.shape[1] // count

    def columns(k):
        return pl.ds(pl.multiple_of(place_ref[k] * width, width), width)

    def fetch(k):
        return pltpu.make_async_copy(
            tokens_ref.at[:, columns(k)], token_buf.at[:, pl.ds(k * width, width)], in_sem.at[k]
        )

    def put(k):
        return pltpu.make_async_copy(
            grad_buf.at[:, pl.ds(k * width, width)], grad_out.at[:, columns(k)], out_sem.at[k]
        )

    for k in range(count):
        fetch(k).start()
    grads = grads_ref[...]
    at = 0
    for weight_ref, size in zip(weight_refs, sizes):
        for j in range(0, size, 4):
            grad_buf[:, pl.ds((at + j) * width, 4 * width)] = lax.dot_general(
                grads,
                weight_ref[pl.ds(j * width, 4 * width), :],
                (((1,), (1,)), ((), ())),
                preferred_element_type=F32,
            ).astype(BF16)
            for k in range(at + j, at + j + 4):
                put(k).start()
        at += size
    for k in range(count):
        fetch(k).wait()
    total, at = None if first else sum_ref[...], 0
    for weight_ref, size in zip(weight_refs, sizes):
        term = jnp.dot(
            token_buf[:, pl.ds(at * width, size * width)],
            weight_ref[...],
            preferred_element_type=F32,
        )
        total = term if total is None else total + term
        at += size
    sum_out[...] = total.astype(sum_out.dtype)
    for k in range(count):
        put(k).wait()


def project(tokens, grads, weights, place, state, last, span=1):
    rows, heads = grads.shape
    tokens = pltpu.with_memory_space_constraint(tokens, pltpu.HBM)
    width = tokens.shape[1] // (NY * NX * NZ)
    sizes = tuple(w.shape[0] // width for w in weights)
    count = sum(sizes)
    first = state is None
    whole = pl.BlockSpec(memory_space=pltpu.VMEM)
    n_in = 3 + len(weights)
    return pl.pallas_call(
        functools.partial(project_kernel, sizes, first),
        in_specs=[pl.BlockSpec(memory_space=pltpu.SMEM), HBM, whole]
        + [whole] * len(weights)
        + ([] if first else [whole, HBM]),
        out_specs=(whole, HBM),
        out_shape=(
            jax.ShapeDtypeStruct((rows, heads), BF16 if last else F32),
            pltpu.HBM(tokens.shape, BF16),
        ),
        scratch_shapes=[
            pltpu.VMEM((rows, count * width), BF16),
            pltpu.VMEM((rows, count * width), BF16),
            pltpu.SemaphoreType.DMA((count,)),
            pltpu.SemaphoreType.DMA((count,)),
        ],
        input_output_aliases={} if first else {n_in + 1: 1},
        compiler_params=pltpu.CompilerParams(vmem_limit_bytes=10 << 20),
        cost_estimate=pl.CostEstimate(
            flops=span * 4 * rows * heads * count * width,
            bytes_accessed=count * width * (rows * 4 + heads * 2),
            transcendentals=0,
        ),
        name="project",
    )(place, tokens, grads, *weights, *(() if first else state))


def outer_kernel(plan_ref, rank_ref, near_ref, far_ref, inner_ref, *refs):
    states, (new_ref, mom_ref) = refs[:-2], refs[-2:]
    groups, width = 2 * len(states), mom_ref.shape[1]
    rank = rank_ref[0]
    for b in range(groups):
        head = b ^ rank
        columns = pl.ds(pl.multiple_of(head * width, width), width)
        anchor, momentum = states[b // 2][b % 2, 0], states[b // 2][b % 2, 1]
        mean = (near_ref[:, columns] + far_ref[:, columns]) / groups
        pseudo = anchor - mean
        following = momentum_coef * momentum + pseudo
        outer = anchor - outer_rate * (pseudo + momentum_coef * following)
        synced = jnp.full(outer.shape, plan_ref[head], jnp.int32) > 0
        new_ref[:, columns] = jnp.where(synced, outer, inner_ref[:, columns]).astype(BF16)
        if b == 0:
            mom_ref[...] = jnp.where(synced, following, momentum)


def outer_step(plan, rank, near, far, inner, state):
    smem = pl.BlockSpec(memory_space=pltpu.SMEM)
    whole = pl.BlockSpec(memory_space=pltpu.VMEM)
    return pl.pallas_call(
        outer_kernel,
        in_specs=[smem, smem] + [whole] * (3 + len(state)),
        out_specs=(whole, whole),
        out_shape=(
            jax.ShapeDtypeStruct(inner.shape, BF16),
            jax.ShapeDtypeStruct(state[0].shape[2:], F32),
        ),
        compiler_params=pltpu.CompilerParams(vmem_limit_bytes=4 << 20),
        name="outer_step",
    )(plan, rank, near, far, inner, *state)


def local(acts, out_grad, weights, anchor, momentum, plan):
    tokens, grads_out, local_weight = acts[0], out_grad[0], weights[0]
    rows, depth = tokens.shape
    heads = grads_out.shape[1]
    total_tokens = rows * NY * NX * NZ
    inner_rate = 1.0 / math.sqrt(total_tokens * depth)
    z = lax.axis_index("z")
    rank = lax.axis_index(REP)
    part = depth // SUB
    sub = ("y", "xl")

    width = part // NZ
    after = lambda x, *others: lax.optimization_barrier((x, *others))[0]

    width = part // NZ
    after = lambda x, *others: lax.optimization_barrier((x, *others))[0]

    beside = shift_x(local_weight)
    moved = [local_weight, beside]
    for dy in range(1, NY):
        moved += [shift_y(local_weight, dy), shift_y(beside, dy)]
    block = [jnp.concatenate(moved[:NY]), jnp.concatenate(moved[NY:])]

    place = jnp.stack([(z + d) % NZ for d in range(NZ)]).astype(jnp.int32)
    first, second = sort_tokens(tokens, grads_out, place)
    block, first = lax.optimization_barrier((block, first))
    first = lax.all_to_all(first, sub, 0, 0)

    y, x = lax.axis_index("y"), lax.axis_index("xl")

    def places(*shifts):
        members = [(y - v) % NY * NX + (x ^ c) for v in range(NY) for c in range(NX)]
        at = [member * NZ + (z + dz) % NZ for dz in shifts for member in members]
        return jnp.stack(at).astype(jnp.int32)

    def add(carry, k, pieces, span=1, last=False):
        at = places(k) if k in (0, 4) else places(-k, k)
        return project(tokens, grads_out, pieces, at, carry, last, span)

    right, left = ([[w] for w in block] for _ in range(2))
    carry = add(None, 0, block)
    for k in (1, 2):
        for h in range(2):
            right[h].append(shift_z(right[h][-1], 1))
            left[h].append(shift_z(left[h][-1], -1))
        pieces = [right[0][k], right[1][k], left[0][k], left[1][k]]
        if k == 1:
            carry = add(carry, 1, pieces, 5)
    step3 = [None] * 4
    step3[0], step3[3] = shift_z(pieces[0], 1), shift_z(pieces[3], -1)
    first, _, pieces = lax.optimization_barrier((first, carry[0], pieces))
    second = lax.all_to_all(after(second, first), sub, 0, 0)

    def terms(tokens, span, *distances):
        s = 0 if distances[0] in STAGES[0] else 1
        at = STAGES[s].index(distances[0]) + (heads // width if s == 0 else 0)
        return partial_grad(tokens, first, heads, width, at, len(distances), span)

    half = width // 2
    middle, ahead, back = terms(first, 5, 4, 3, 5)
    up, down = shift_z(middle[:half], 1), shift_z(middle[half:], -1)
    state = after(jnp.stack([anchor, momentum]), middle)
    states = jnp.stack([state, shift_core(state)])
    up = jnp.concatenate([ahead[:half] + up, ahead[half:]])
    down = jnp.concatenate([back[:half], back[half:] + down])
    up, down, states, step3 = lax.optimization_barrier((up, down, states, step3))
    step3[1] = shift_z(after(pieces[1], up), 1)
    step3[2] = shift_z(after(pieces[2], down), -1)
    ahead, back = terms(after(first, up, down), 5, 2, 6)
    up, down = shift_z(up, 1), shift_z(down, -1)
    up, down = ahead + up, back + down
    distant = shift_far(after(states, up))
    nearest = terms(second, 5, 1, 7, 0)
    up, down = shift_z(up, 1), shift_z(down, -1)
    up, down = nearest[0] + up, nearest[1] + down
    up, down, distant, step3 = lax.optimization_barrier((up, down, distant, step3))
    up, down = shift_z(up, 1), shift_z(down, -1)
    step4 = [shift_z(step3[0], 1), shift_z(step3[3], -1)]
    carry = add(carry, 2, pieces, 3)
    up, down, _ = lax.optimization_barrier((up, down, carry[0]))
    inner = local_weight.astype(F32) - inner_rate * (nearest[2] + up + down)
    carry = add(carry, 3, step3)

    near = inner + shift_core(inner)
    far = shift_far(near)
    values, act_grad = add(carry, 4, step4, last=True)
    new_weight, new_momentum = outer_step(
        plan, jnp.reshape(rank, (1,)).astype(jnp.int32), near, far, inner, [states, distant]
    )
    return values[None], act_grad[None], new_weight[None], new_momentum


def solution(mesh):
    fine = Mesh(mesh.devices.reshape(2, 2, NY, NX, NZ), ("xh", "core", "y", "xl", "z"))
    placed = (
        P(REP, FSDP, None),
        P(REP, FSDP, None),
        P(REP, FSDP, None),
        P(FSDP, REP),
        P(FSDP, REP),
        P(),
    )
    return jax.shard_map(
        local,
        mesh=fine,
        in_specs=placed,
        out_specs=(
            P(REP, FSDP, None),
            P(REP, FSDP, None),
            P(REP, FSDP, None),
            P(FSDP, REP),
        ),
        check_vma=False,
    )
```

```python
import functools
import math

import jax
import jax.numpy as jnp
from jax import lax
from jax.experimental import pallas as pl
from jax.experimental.pallas import tpu as pltpu
from jax.sharding import Mesh, PartitionSpec as P

outer_rate = 0.7
momentum_coef = 0.9
NY, NX, NZ = 4, 2, 8
SUB = NY * NX
REP = ("xh", "core")
FSDP = ("y", "xl", "z")
HBM = pl.BlockSpec(memory_space=pltpu.HBM)
F32 = jnp.float32
BF16 = jnp.bfloat16
STAGES = ((4, 3, 5, 2, 6), (1, 7, 0))


def shift_z(x, dz):
    return lax.ppermute(x, "z", [(i, (i + dz) % NZ) for i in range(NZ)])


def shift_y(x, dy):
    return lax.ppermute(x, "y", [(i, (i + dy) % NY) for i in range(NY)])


def shift_x(x):
    return lax.ppermute(x, "xl", [(0, 1), (1, 0)])


def shift_core(x):
    return lax.ppermute(x, "core", [(0, 1), (1, 0)])


def shift_far(x):
    return lax.ppermute(x, "xh", [(0, 1), (1, 0)])


def sort_kernel(place_ref, tokens_ref, grads_ref, *refs):
    n = len(STAGES)
    outs, (tokens_buf, grads_buf), bufs, (in_sem, out_sem) = (
        refs[:n], refs[n : n + 2], refs[n + 2 : 2 * n + 2], refs[2 * n + 2 :]
    )
    heads = grads_ref.shape[1]
    part = tokens_buf.shape[2]
    width = part // NZ
    fetches = [pltpu.make_async_copy(grads_ref, grads_buf, in_sem.at[SUB])]
    for j in range(SUB):
        fetches.append(
            pltpu.make_async_copy(
                tokens_ref.at[:, pl.ds(j * part, part)], tokens_buf.at[j], in_sem.at[j]
            )
        )
    for fetch in fetches:
        fetch.start()
    fetches[0].wait()
    puts = []
    for j in range(SUB):
        fetches[1 + j].wait()
        bufs[0][j, :, :heads] = grads_buf[...]
        for s, stage in enumerate(STAGES):
            start = heads if s == 0 else 0
            for i, d in enumerate(stage):
                source = pl.multiple_of(place_ref[d] * width, width)
                bufs[s][j, :, pl.ds(start + i * width, width)] = tokens_buf[
                    j, :, pl.ds(source, width)
                ]
            put = pltpu.make_async_copy(bufs[s].at[j], outs[s].at[j], out_sem.at[s, j])
            put.start()
            puts.append(put)
    for put in puts:
        put.wait()


def sort_tokens(tokens, grads, place):
    tokens = pltpu.with_memory_space_constraint(tokens, pltpu.HBM)
    grads = pltpu.with_memory_space_constraint(grads, pltpu.HBM)
    rows, depth = tokens.shape
    heads = grads.shape[1]
    part = depth // SUB
    width = part // NZ
    sizes = [len(stage) * width + (heads if s == 0 else 0) for s, stage in enumerate(STAGES)]
    return pl.pallas_call(
        sort_kernel,
        in_specs=[pl.BlockSpec(memory_space=pltpu.SMEM), HBM, HBM],
        out_specs=(HBM,) * len(sizes),
        out_shape=tuple(pltpu.HBM((SUB, rows, n), tokens.dtype) for n in sizes),
        scratch_shapes=[
            pltpu.VMEM((SUB, rows, part), tokens.dtype),
            pltpu.VMEM((rows, heads), tokens.dtype),
            *[pltpu.VMEM((SUB, rows, n), tokens.dtype) for n in sizes],
            pltpu.SemaphoreType.DMA((SUB + 1,)),
            pltpu.SemaphoreType.DMA((len(sizes), SUB)),
        ],
        compiler_params=pltpu.CompilerParams(vmem_limit_bytes=12 << 20),
        cost_estimate=pl.CostEstimate(
            flops=0, bytes_accessed=8 * rows * (depth + heads), transcendentals=0
        ),
        name="sort_tokens",
    )(place, tokens, grads)


def grad_kernel(tokens_ref, grads_ref, out_ref):
    members, rows, width = tokens_ref.shape
    heads = grads_ref.shape[2]
    out_ref[0] = lax.dot_general(
        tokens_ref[...].reshape(members * rows, width),
        grads_ref[...].reshape(members * rows, heads),
        (((0,), (0,)), ((), ())),
        preferred_element_type=F32,
    )


def partial_grad(tokens, first, heads, width, at, count, span):
    members, rows, _ = tokens.shape
    return pl.pallas_call(
        grad_kernel,
        grid=(count,),
        in_specs=[
            pl.BlockSpec((members, rows, width), lambda d: (0, 0, d + at)),
            pl.BlockSpec((members, rows, heads), lambda d: (0, 0, 0)),
        ],
        out_specs=pl.BlockSpec((1, width, heads), lambda d: (d, 0, 0)),
        out_shape=jax.ShapeDtypeStruct((count, width, heads), F32),
        compiler_params=pltpu.CompilerParams(vmem_limit_bytes=8 << 20),
        cost_estimate=pl.CostEstimate(
            flops=span * 2 * members * rows * count * width * heads,
            bytes_accessed=0,
            transcendentals=0,
        ),
        name="partial_grad",
    )(tokens, first)


def project_kernel(sizes, first, place_ref, tokens_ref, grads_ref, *refs):
    n = len(sizes)
    weight_refs, refs = refs[:n], refs[n:]
    if not first:
        sum_ref, _, refs = refs[0], refs[1], refs[2:]
    sum_out, grad_out, token_buf, grad_buf, in_sem, out_sem = refs
    count = sum(sizes)
    width = token_buf.shape[1] // count

    def columns(k):
        return pl.ds(pl.multiple_of(place_ref[k] * width, width), width)

    def fetch(k):
        return pltpu.make_async_copy(
            tokens_ref.at[:, columns(k)], token_buf.at[:, pl.ds(k * width, width)], in_sem.at[k]
        )

    def put(k):
        return pltpu.make_async_copy(
            grad_buf.at[:, pl.ds(k * width, width)], grad_out.at[:, columns(k)], out_sem.at[k]
        )

    for k in range(count):
        fetch(k).start()
    grads = grads_ref[...]
    at = 0
    for weight_ref, size in zip(weight_refs, sizes):
        for j in range(0, size, 4):
            grad_buf[:, pl.ds((at + j) * width, 4 * width)] = lax.dot_general(
                grads,
                weight_ref[pl.ds(j * width, 4 * width), :],
                (((1,), (1,)), ((), ())),
                preferred_element_type=F32,
            ).astype(BF16)
            for k in range(at + j, at + j + 4):
                put(k).start()
        at += size
    for k in range(count):
        fetch(k).wait()
    total, at = None if first else sum_ref[...], 0
    for weight_ref, size in zip(weight_refs, sizes):
        term = jnp.dot(
            token_buf[:, pl.ds(at * width, size * width)],
            weight_ref[...],
            preferred_element_type=F32,
        )
        total = term if total is None else total + term
        at += size
    sum_out[...] = total.astype(sum_out.dtype)
    for k in range(count):
        put(k).wait()


def project(tokens, grads, weights, place, state, last, span=1):
    rows, heads = grads.shape
    tokens = pltpu.with_memory_space_constraint(tokens, pltpu.HBM)
    width = tokens.shape[1] // (NY * NX * NZ)
    sizes = tuple(w.shape[0] // width for w in weights)
    count = sum(sizes)
    first = state is None
    whole = pl.BlockSpec(memory_space=pltpu.VMEM)
    n_in = 3 + len(weights)
    return pl.pallas_call(
        functools.partial(project_kernel, sizes, first),
        in_specs=[pl.BlockSpec(memory_space=pltpu.SMEM), HBM, whole]
        + [whole] * len(weights)
        + ([] if first else [whole, HBM]),
        out_specs=(whole, HBM),
        out_shape=(
            jax.ShapeDtypeStruct((rows, heads), BF16 if last else F32),
            pltpu.HBM(tokens.shape, BF16),
        ),
        scratch_shapes=[
            pltpu.VMEM((rows, count * width), BF16),
            pltpu.VMEM((rows, count * width), BF16),
            pltpu.SemaphoreType.DMA((count,)),
            pltpu.SemaphoreType.DMA((count,)),
        ],
        input_output_aliases={} if first else {n_in + 1: 1},
        compiler_params=pltpu.CompilerParams(vmem_limit_bytes=10 << 20),
        cost_estimate=pl.CostEstimate(
            flops=span * 4 * rows * heads * count * width,
            bytes_accessed=count * width * (rows * 4 + heads * 2),
            transcendentals=0,
        ),
        name="project",
    )(place, tokens, grads, *weights, *(() if first else state))


def outer_kernel(plan_ref, rank_ref, near_ref, far_ref, inner_ref, *refs):
    states, (new_ref, mom_ref) = refs[:-2], refs[-2:]
    groups, width = 2 * len(states), mom_ref.shape[1]
    rank = rank_ref[0]
    for b in range(groups):
        head = b ^ rank
        columns = pl.ds(pl.multiple_of(head * width, width), width)
        anchor, momentum = states[b // 2][b % 2, 0], states[b // 2][b % 2, 1]
        mean = (near_ref[:, columns] + far_ref[:, columns]) / groups
        pseudo = anchor - mean
        following = momentum_coef * momentum + pseudo
        outer = anchor - outer_rate * (pseudo + momentum_coef * following)
        synced = jnp.full(outer.shape, plan_ref[head], jnp.int32) > 0
        new_ref[:, columns] = jnp.where(synced, outer, inner_ref[:, columns]).astype(BF16)
        if b == 0:
            mom_ref[...] = jnp.where(synced, following, momentum)


def outer_step(plan, rank, near, far, inner, state):
    smem = pl.BlockSpec(memory_space=pltpu.SMEM)
    whole = pl.BlockSpec(memory_space=pltpu.VMEM)
    return pl.pallas_call(
        outer_kernel,
        in_specs=[smem, smem] + [whole] * (3 + len(state)),
        out_specs=(whole, whole),
        out_shape=(
            jax.ShapeDtypeStruct(inner.shape, BF16),
            jax.ShapeDtypeStruct(state[0].shape[2:], F32),
        ),
        compiler_params=pltpu.CompilerParams(vmem_limit_bytes=4 << 20),
        name="outer_step",
    )(plan, rank, near, far, inner, *state)


def local(acts, out_grad, weights, anchor, momentum, plan):
    tokens, grads_out, local_weight = acts[0], out_grad[0], weights[0]
    rows, depth = tokens.shape
    heads = grads_out.shape[1]
    total_tokens = rows * NY * NX * NZ
    inner_rate = 1.0 / math.sqrt(total_tokens * depth)
    z = lax.axis_index("z")
    rank = lax.axis_index(REP)
    part = depth // SUB
    sub = ("y", "xl")

    width = part // NZ
    after = lambda x, *others: lax.optimization_barrier((x, *others))[0]

    width = part // NZ
    after = lambda x, *others: lax.optimization_barrier((x, *others))[0]

    beside = shift_x(local_weight)
    moved = [local_weight, beside]
    for dy in range(1, NY):
        moved += [shift_y(local_weight, dy), shift_y(beside, dy)]
    block = [jnp.concatenate(moved[:NY]), jnp.concatenate(moved[NY:])]

    place = jnp.stack([(z + d) % NZ for d in range(NZ)]).astype(jnp.int32)
    first, second = sort_tokens(tokens, grads_out, place)
    block, first = lax.optimization_barrier((block, first))
    first = lax.all_to_all(first, sub, 0, 0)

    y, x = lax.axis_index("y"), lax.axis_index("xl")

    def places(*shifts):
        members = [(y - v) % NY * NX + (x ^ c) for v in range(NY) for c in range(NX)]
        at = [member * NZ + (z + dz) % NZ for dz in shifts for member in members]
        return jnp.stack(at).astype(jnp.int32)

    def add(carry, k, pieces, span=1, last=False):
        at = places(k) if k in (0, 4) else places(-k, k)
        return project(tokens, grads_out, pieces, at, carry, last, span)

    right, left = ([[w] for w in block] for _ in range(2))
    carry = add(None, 0, block)
    for k in (1, 2):
        for h in range(2):
            right[h].append(shift_z(right[h][-1], 1))
            left[h].append(shift_z(left[h][-1], -1))
        pieces = [right[0][k], right[1][k], left[0][k], left[1][k]]
        if k == 1:
            carry = add(carry, 1, pieces, 5)
    step3 = [None] * 4
    step3[0], step3[2] = shift_z(pieces[0], 1), shift_z(pieces[2], -1)
    first, _, pieces = lax.optimization_barrier((first, carry[0], pieces))
    second = lax.all_to_all(after(second, first), sub, 0, 0)

    def terms(tokens, span, *distances):
        s = 0 if distances[0] in STAGES[0] else 1
        at = STAGES[s].index(distances[0]) + (heads // width if s == 0 else 0)
        return partial_grad(tokens, first, heads, width, at, len(distances), span)

    half = width // 2
    middle, ahead, back = terms(first, 5, 4, 3, 5)
    up, down = shift_z(middle[:half], 1), shift_z(middle[half:], -1)
    state = after(jnp.stack([anchor, momentum]), middle)
    states = jnp.stack([state, shift_core(state)])
    up = jnp.concatenate([ahead[:half] + up, ahead[half:]])
    down = jnp.concatenate([back[:half], back[half:] + down])
    up, down, states, step3 = lax.optimization_barrier((up, down, states, step3))
    step3[1] = shift_z(after(pieces[1], up), 1)
    step3[3] = shift_z(after(pieces[3], down), -1)
    ahead, back = terms(after(first, up, down), 5, 2, 6)
    up, down = shift_z(up, 1), shift_z(down, -1)
    up, down = ahead + up, back + down
    distant = shift_far(after(states, up))
    nearest = terms(second, 5, 1, 7, 0)
    up, down = shift_z(up, 1), shift_z(down, -1)
    up, down = nearest[0] + up, nearest[1] + down
    up, down, distant, step3 = lax.optimization_barrier((up, down, distant, step3))
    up, down = shift_z(up, 1), shift_z(down, -1)
    step4 = [shift_z(step3[0], 1), shift_z(step3[3], -1)]
    carry = add(carry, 2, pieces, 3)
    up, down, _ = lax.optimization_barrier((up, down, carry[0]))
    inner = local_weight.astype(F32) - inner_rate * (nearest[2] + up + down)
    carry = add(carry, 3, step3)

    near = inner + shift_core(inner)
    far = shift_far(near)
    values, act_grad = add(carry, 4, step4, last=True)
    new_weight, new_momentum = outer_step(
        plan, jnp.reshape(rank, (1,)).astype(jnp.int32), near, far, inner, [states, distant]
    )
    return values[None], act_grad[None], new_weight[None], new_momentum


def solution(mesh):
    fine = Mesh(mesh.devices.reshape(2, 2, NY, NX, NZ), ("xh", "core", "y", "xl", "z"))
    placed = (
        P(REP, FSDP, None),
        P(REP, FSDP, None),
        P(REP, FSDP, None),
        P(FSDP, REP),
        P(FSDP, REP),
        P(),
    )
    return jax.shard_map(
        local,
        mesh=fine,
        in_specs=placed,
        out_specs=(
            P(REP, FSDP, None),
            P(REP, FSDP, None),
            P(REP, FSDP, None),
            P(FSDP, REP),
        ),
        check_vma=False,
    )
```
